768 devices in a mesh: row: 12 (over z), col: 64 (over y, x, core).
Axes of the slice: x: 4, y: 8, z: 12, core: 2. Of those that a mesh axis runs over, the one named last changes fastest.
Arguments:
- momentum: float32 [6144, 28672], P('row', 'col'), may hold values from -600 to 600
- gradient: bfloat16 [6144, 28672], P('row', 'col'), may hold values from -600 to 600
- right_factor: float32 [28672, 512], P('col'), may hold values from -6 to 6
Outputs:
- momentum_next: float32 [6144, 28672], P('row', 'col')
- right_next: float32 [28672, 512], P('col')
- update: bfloat16 [6144, 28672], P('row', 'col')
The draws below stay inside these ranges and needn't reach their ends.
All inputs are finite; a program needn't handle non-finite values.
Results may differ from the reference program's by a relative error of at most 0.0015.
Values sent between devices are 32-bit elements; how exact they have to be, the bound alone decides.
No kernel may reach another device: no remote copies, remote signals or barrier semaphores. Data moves between devices by JAX's collectives and lax.ppermute only.
A program may use at most 32 MiB of HBM per device.

```python
import jax
import jax.numpy as jnp
from jax import lax

COLS = 28672
RANK = 512
ROWS = 6144


def scales(key):
    key_rows, key_cols = jax.random.split(key)
    row_scale = 10.0 ** jax.random.uniform(key_rows, (ROWS, 1), jnp.float32)
    ramp = 1.0 + 2.0 * jnp.arange(COLS, dtype=jnp.float32)[None, :] / COLS
    col_scale = 10.0 ** jax.random.uniform(key_cols, (1, COLS), jnp.float32) * ramp
    return row_scale * col_scale


def draw_momentum(key, part):
    key = jax.random.fold_in(key, 11)
    key_scale, key_base = jax.random.split(key, 2)
    base = jax.random.normal(key_base, (ROWS, COLS), jnp.float32)
    base = jnp.clip(base, -6.0, 6.0)
    return 0.3 * base * scales(key_scale)


def draw_gradient(key, part):
    key = jax.random.fold_in(key, 23)
    key_scale, key_base = jax.random.split(key, 2)
    base = jax.random.normal(key_base, (ROWS, COLS), jnp.float32)
    base = jnp.clip(base, -6.0, 6.0)
    return (0.3 * base * scales(key_scale)).astype(jnp.bfloat16)


def levels(key, dims, pieces, low, top_value):
    loudness = 1.0
    for axis_at, parts in pieces:
        draws = jax.random.uniform(jax.random.fold_in(jax.random.fold_in(key, 6), axis_at), (parts,), jnp.float32, low / len(pieces), top_value / len(pieces))
        loudness = loudness * jnp.repeat(jnp.exp(draws), dims[axis_at] // parts).reshape((-1,) + (1,) * (len(dims) - 1 - axis_at))
    return loudness


def gaussian(key, dims, scale, reach, pieces=(), held_as=jnp.bfloat16):
    array = scale * jax.random.normal(key, dims, jnp.float32)
    if pieces:
        array = array * levels(key, dims, pieces, -0.22, 0.18)
    return jnp.clip(array, -reach, reach).astype(held_as)


def setup_inputs(seed: int = 0) -> dict:
    keys = jax.random.split(jax.random.key(seed), 4)
    return {
        "momentum": draw_momentum(jax.random.fold_in(keys[3], 71), 0),
        "gradient": draw_gradient(jax.random.fold_in(keys[3], 71), 0),
        "right_factor": gaussian(keys[2], (COLS, RANK), 1.0, 6.0, ((0, 64),), jnp.float32),
    }


def reference(momentum, gradient, right_factor):
    high = lax.Precision.HIGHEST
    blend = momentum + gradient.astype(jnp.float32)
    left = jnp.dot(blend.astype(jnp.float32), right_factor.astype(jnp.float32), preferred_element_type=jnp.float32, precision=high)
    gram = jnp.dot(left.T.astype(jnp.float32), left.astype(jnp.float32), preferred_element_type=jnp.float32, precision=high)
    lower = jnp.linalg.cholesky(gram)
    ortho = jax.scipy.linalg.solve_triangular(lower, left.T, lower=True).T
    right = jnp.dot(blend.T.astype(jnp.float32), ortho.astype(jnp.float32), preferred_element_type=jnp.float32, precision=high)
    meansq = lax.optimization_barrier(jnp.sum(right * right, axis=0)) / COLS
    right_next = right * lax.rsqrt(meansq + 1e-06)
    momentum_next = blend - 0.05 * jnp.dot(ortho.astype(jnp.float32), right.T.astype(jnp.float32), preferred_element_type=jnp.float32, precision=high)
    update = (jnp.sqrt(jnp.float32(ROWS) / RANK) * jnp.dot(ortho.astype(jnp.float32), right_next.T.astype(jnp.float32), preferred_element_type=jnp.float32, precision=high)).astype(jnp.bfloat16)
    return (momentum_next, right_next, update)
```

```python
import jax
import jax.numpy as jnp
from jax import lax
from jax.sharding import Mesh, PartitionSpec as P

HIGHEST = lax.Precision.HIGHEST
HIGH = lax.Precision.HIGH
CHIPS = ("y", "x")


def dot(a, b, dims, precision=HIGHEST):
    return lax.dot_general(
        a, b, ((dims[:1], dims[1:]), ((), ())), precision=precision, preferred_element_type=jnp.float32
    )


def exchange(blocks, axis):
    return lax.all_to_all(blocks, axis, 0, 0, tiled=True)


def spread(block, axis):
    copies = jnp.broadcast_to(block[None], (lax.axis_size(axis),) + block.shape)
    return exchange(copies, axis).reshape((-1,) + block.shape[1:])


def gather_columns(block):
    return spread(spread(block, CHIPS), "core")


def scatter_columns(whole):
    half = jnp.sum(exchange(whole.reshape((2, -1) + whole.shape[1:]), "core"), axis=0)
    parts = half.reshape((lax.axis_size(CHIPS), -1) + half.shape[1:])
    return jnp.sum(exchange(parts, CHIPS), axis=0)


def inverse_factor(gram):
    lower = jnp.linalg.cholesky(gram)
    return jax.scipy.linalg.solve_triangular(lower, jnp.eye(gram.shape[0], dtype=gram.dtype), lower=True)


def shards(momentum, gradient, right_factor):
    rank = right_factor.shape[1]
    blend = momentum + gradient.astype(jnp.float32)
    left = gather_columns(scatter_columns(dot(right_factor, blend, (0, 1))))
    crossed = lax.psum(dot(blend, left, (0, 1)), "row")
    position = lax.axis_index("core") * lax.axis_size(CHIPS) + lax.axis_index(CHIPS)
    width = rank // (2 * lax.axis_size(CHIPS))
    mine = lax.dynamic_slice_in_dim(left, position * width, width, 0)
    piece = dot(mine, left, (1, 1))
    piece = jnp.sum(exchange(jnp.broadcast_to(piece[None], (lax.axis_size("row"),) + piece.shape), "row"), axis=0)
    gram = gather_columns(piece)
    inverse = inverse_factor(gram)
    right = dot(crossed, inverse, (1, 1))
    squares = jnp.sum(right * right, axis=0)
    squares = jnp.sum(spread(squares[None], CHIPS + ("core",)), axis=0)
    total_cols = right.shape[0] * lax.axis_size(CHIPS + ("core",))
    total_rows = blend.shape[0] * lax.axis_size("row")
    right_next = right * lax.rsqrt(squares / total_cols + 1e-06)
    ortho = dot(left, inverse, (0, 1))
    momentum_next = blend - 0.05 * dot(ortho, right, (1, 1))
    factor = jnp.sqrt(jnp.float32(total_rows) / rank)
    update = (factor * dot(ortho, right_next, (1, 1))).astype(jnp.bfloat16)
    return (momentum_next, right_next, update)


def solution(mesh):
    rows, cols = mesh.devices.shape
    split = Mesh(mesh.devices.reshape(rows, 8, 4, 2), ("row", "y", "x", "core"))
    col = ("y", "x", "core")
    return jax.shard_map(
        shards,
        mesh=split,
        in_specs=(P("row", col), P("row", col), P(col, None)),
        out_specs=(P("row", col), P(col, None), P("row", col)),
        check_vma=False,
    )
```

```python
import jax
import jax.numpy as jnp
from jax import lax
from jax.experimental import pallas as pl
from jax.experimental.pallas import tpu as pltpu
from jax.sharding import Mesh, PartitionSpec as P

HIGHEST = lax.Precision.HIGHEST
HIGH = lax.Precision.HIGH
CHIPS = ("y", "x")
TILE = 8
LANES = 128


def dot(a, b, dims, precision=HIGHEST):
    return lax.dot_general(
        a, b, ((dims[:1], dims[1:]), ((), ())), precision=precision, preferred_element_type=jnp.float32
    )


def exchange(blocks, axis):
    return lax.all_to_all(blocks, axis, 0, 0, tiled=True)


def spread(block, axis):
    copies = jnp.broadcast_to(block[None], (lax.axis_size(axis),) + block.shape)
    return exchange(copies, axis).reshape((-1,) + block.shape[1:])


def scatter(whole, axis):
    return jnp.sum(exchange(whole.reshape((lax.axis_size(axis), -1) + whole.shape[1:]), axis), axis=0)


def gather_columns(block):
    return spread(spread(block, CHIPS), "core")


def block_inverse(block):
    shape = (TILE, LANES)
    row = lax.broadcasted_iota(jnp.int32, shape, 0)
    lane = lax.broadcasted_iota(jnp.int32, shape, 1)
    at_row = [row == j for j in range(TILE)]

    def down(x, j):
        return jnp.broadcast_to(x[j : j + 1, :], shape)

    def along(x, k):
        return jnp.broadcast_to(x[:, k : k + 1], shape)

    def combine(columns, rows):
        terms = [c * r for c, r in zip(columns, rows)]
        while len(terms) > 1:
            terms = [terms[i] + terms[i + 1] for i in range(0, len(terms), 2)]
        return terms[0]

    count = LANES // TILE
    strips = [block[TILE * u : TILE * (u + 1), :] for u in range(count)]
    done = []
    for t in range(count):
        first = TILE * t
        inside = (lane >= first) & (lane < first + TILE)
        strip = strips[t]
        columns = [along(strip, first + j) for j in range(TILE)]
        below = [[along(strips[u], first + j) for j in range(TILE)] for u in range(t + 1, count)]
        rows = jnp.where(inside, jnp.where(lane - first == row, 1.0, 0.0), strip)
        rows = [down(rows, j) for j in range(TILE)]
        pivots = jnp.ones(shape, jnp.float32)
        lower = [jnp.where(at_row[m], 1.0, 0.0) for m in range(TILE)]
        for j in range(TILE):
            pivot_row = [down(columns[m], j) for m in range(TILE)]
            inverse = 1.0 / pivot_row[j]
            pivots = jnp.where(at_row[j], pivot_row[j], pivots)
            for m in range(j):
                lower[m] = jnp.where(at_row[j], pivot_row[m], lower[m])
            ratio = columns[j] * inverse
            columns = [
                jnp.where(at_row[j], inverse, -ratio)
                if m == j
                else jnp.where(at_row[j], pivot_row[m] * inverse, columns[m] - ratio * pivot_row[m])
                for m in range(TILE)
            ]
        done.append(jnp.where(lane < first + TILE, combine(lower, rows) * lax.rsqrt(pivots), 0.0))
        solved = combine(columns, rows)
        solved = [down(solved, j) for j in range(TILE)]
        for u in range(t + 1, count):
            strips[u] = jnp.where(inside, 0.0, strips[u]) - combine(below[u - t - 1], solved)
    return jnp.concatenate(done, axis=0)


def inverse_factor_kernel(gram_ref, inverse_ref, work_ref):
    count = gram_ref.shape[0] // LANES
    work_ref[...] = gram_ref[...]
    inverse_ref[...] = jnp.zeros_like(inverse_ref)

    def at(i):
        return slice(LANES * i, LANES * (i + 1))

    for b in range(count):
        inverse = block_inverse(work_ref[at(b), at(b)])
        inverse_ref[at(b), at(b)] = inverse
        before, after = slice(0, LANES * b), slice(LANES * (b + 1), LANES * count)
        if b:
            inverse_ref[at(b), before] = dot(inverse, work_ref[at(b), before], (1, 0))
        if b == count - 1:
            break
        strip = dot(inverse, work_ref[at(b), after], (1, 0))
        for i in range(b + 1, count):
            offset = LANES * (i - b - 1)
            factor = strip[:, offset : offset + LANES]
            rest = slice(LANES * i, LANES * count)
            work_ref[at(i), rest] = work_ref[at(i), rest] - dot(factor, strip[:, offset:], (0, 0))
            work_ref[at(i), at(b)] = -dot(factor, inverse, (0, 0))
            if b:
                work_ref[at(i), before] = work_ref[at(i), before] - dot(
                    factor, inverse_ref[at(b), before], (0, 0)
                )


def inverse_factor(gram):
    return pl.pallas_call(
        inverse_factor_kernel,
        out_shape=jax.ShapeDtypeStruct(gram.shape, jnp.float32),
        in_specs=[pl.BlockSpec(memory_space=pltpu.VMEM)],
        out_specs=pl.BlockSpec(memory_space=pltpu.VMEM),
        scratch_shapes=[pltpu.VMEM(gram.shape, jnp.float32)],
        compiler_params=pltpu.CompilerParams(vmem_limit_bytes=16 * 1024 * 1024),
        cost_estimate=pl.CostEstimate(flops=1 << 30, bytes_accessed=1 << 26, transcendentals=0),
    )(gram)


def correct_kernel(left_ref, inverse_ref, right_ref, momentum_ref, gradient_ref, ortho_ref, next_ref):
    ortho = dot(inverse_ref[...], left_ref[...], (1, 0))
    ortho_ref[...] = ortho
    blend = momentum_ref[...] + gradient_ref[...].astype(jnp.float32)
    next_ref[...] = blend - 0.05 * dot(right_ref[...], ortho, (1, 0))


def correct(left, inverse, right, momentum, gradient):
    vmem = pl.BlockSpec(memory_space=pltpu.VMEM)
    return pl.pallas_call(
        correct_kernel,
        out_shape=(
            jax.ShapeDtypeStruct(left.shape, jnp.float32),
            jax.ShapeDtypeStruct(momentum.shape, jnp.float32),
        ),
        in_specs=[vmem] * 5,
        out_specs=(vmem, vmem),
        compiler_params=pltpu.CompilerParams(vmem_limit_bytes=24 * 1024 * 1024),
        cost_estimate=pl.CostEstimate(flops=1 << 33, bytes_accessed=1 << 23, transcendentals=0),
    )(left, inverse, right, momentum, gradient)


def sum_rows(block):
    share = lax.psum_scatter(block, "row", scatter_dimension=0, tiled=True)
    return lax.all_gather(share, "row", axis=0, tiled=True)


def shards(momentum, gradient, right_factor):
    rank = right_factor.shape[1]
    col = CHIPS + ("core",)
    blend = momentum + gradient.astype(jnp.float32)
    left = gather_columns(scatter(scatter(dot(right_factor, blend, (0, 1)), "core"), CHIPS))
    width = rank // lax.axis_size(col)
    position = lax.axis_index("core") * lax.axis_size(CHIPS) + lax.axis_index(CHIPS)
    mine = lax.dynamic_slice_in_dim(left, position * width, width, 0)
    piece = jnp.sum(spread(dot(mine, left, (1, 1))[None], "row"), axis=0)
    columns = blend.shape[1]
    spare = -columns % (TILE * lax.axis_size("row"))
    crossed = sum_rows(dot(jnp.pad(blend, ((0, 0), (0, spare))), left, (0, 1)))[:columns]
    inverse = inverse_factor(gather_columns(piece))
    right = dot(crossed, inverse, (1, 1))
    squares = jnp.sum(spread(jnp.sum(right * right, axis=0)[None], col), axis=0)
    total_cols = right.shape[0] * lax.axis_size(col)
    total_rows = blend.shape[0] * lax.axis_size("row")
    right_next = right * lax.rsqrt(squares / total_cols + 1e-06)
    ortho, momentum_next = correct(left, inverse, right, momentum.T, gradient.T)
    factor = jnp.sqrt(jnp.float32(total_rows) / rank)
    update = (factor * dot(right_next, ortho, (1, 0), HIGH)).astype(jnp.bfloat16)
    return (momentum_next.T, right_next, update.T)


def solution(mesh):
    rows = mesh.devices.shape[0]
    split = Mesh(mesh.devices.reshape(rows, 8, 4, 2), ("row", "y", "x", "core"))
    col = CHIPS + ("core",)
    return jax.shard_map(
        shards,
        mesh=split,
        in_specs=(P("row", col), P("row", col), P(col, None)),
        out_specs=(P("row", col), P(col, None), P("row", col)),
        check_vma=False,
    )
```

```python
import functools

import jax
import jax.numpy as jnp
from jax import lax
from jax.experimental import pallas as pl
from jax.experimental.pallas import tpu as pltpu
from jax.sharding import Mesh, PartitionSpec as P

HIGHEST = lax.Precision.HIGHEST
HIGH = lax.Precision.HIGH
CHIPS = ("y", "x")
TILE = 8
LANES = 128


def dot(a, b, dims, precision=HIGHEST):
    return lax.dot_general(
        a, b, ((dims[:1], dims[1:]), ((), ())), precision=precision, preferred_element_type=jnp.float32
    )


def exchange(blocks, axis):
    return lax.all_to_all(blocks, axis, 0, 0, tiled=True)


def spread(block, axis):
    copies = jnp.broadcast_to(block[None], (lax.axis_size(axis),) + block.shape)
    return exchange(copies, axis).reshape((-1,) + block.shape[1:])


def scatter(whole, axis):
    return jnp.sum(exchange(whole.reshape((lax.axis_size(axis), -1) + whole.shape[1:]), axis), axis=0)


def gather_columns(block):
    return spread(spread(block, CHIPS), "core")


def block_inverse(block, later):
    shape = (TILE, LANES)
    row = lax.broadcasted_iota(jnp.int32, shape, 0)
    lane = lax.broadcasted_iota(jnp.int32, shape, 1)
    at_row = [row == j for j in range(TILE)]

    def down(x, j):
        return jnp.broadcast_to(x[j : j + 1, :], shape)

    def along(x, k):
        return jnp.broadcast_to(x[:, k : k + 1], shape)

    def combine(columns, rows):
        terms = [c * r for c, r in zip(columns, rows)]
        while len(terms) > 1:
            terms = [terms[i] + terms[i + 1] for i in range(0, len(terms), 2)]
        return terms[0]

    later = list(later)
    count = LANES // TILE
    strips = [block[TILE * u : TILE * (u + 1), :] for u in range(count)]
    done = []
    for t in range(count):
        first = TILE * t
        inside = (lane >= first) & (lane < first + TILE)
        strip = strips[t]
        columns = [along(strip, first + j) for j in range(TILE)]
        rows = jnp.where(inside, jnp.where(lane - first == row, 1.0, 0.0), strip)
        rows = [down(rows, j) for j in range(TILE)]
        pivots = jnp.ones(shape, jnp.float32)
        lower = [jnp.where(at_row[m], 1.0, 0.0) for m in range(TILE)]
        for j in range(0, TILE, 2):
            k = j + 1
            upper_row = [down(columns[m], j) for m in range(TILE)]
            lower_row = [down(columns[m], k) for m in range(TILE)]
            a, b, d = upper_row[j], lower_row[j], lower_row[k]
            scale = 1.0 / (a * d - b * b)
            at_j = jnp.where(at_row[j], -1.0, jnp.where(at_row[k], 0.0, columns[j]))
            at_k = jnp.where(at_row[k], -1.0, jnp.where(at_row[j], 0.0, columns[k]))
            ratio_j = (at_j * d - at_k * b) * scale
            ratio_k = (at_k * a - at_j * b) * scale
            step = b / a
            pivots = jnp.where(at_row[j], a, jnp.where(at_row[k], d - b * step, pivots))
            for m in range(j):
                lower[m] = jnp.where(
                    at_row[j], upper_row[m], jnp.where(at_row[k], lower_row[m] - step * upper_row[m], lower[m])
                )
            lower[j] = jnp.where(at_row[k], -step, lower[j])
            pair = at_row[j] | at_row[k]
            columns = [
                -ratio_j
                if m == j
                else -ratio_k
                if m == k
                else (jnp.where(pair, 0.0, columns[m]) - ratio_j * upper_row[m]) - ratio_k * lower_row[m]
                for m in range(TILE)
            ]
        done.append(jnp.where(lane < first + TILE, combine(lower, rows) * lax.rsqrt(pivots), 0.0))
        solved = combine(columns, rows)
        solved = [down(solved, j) for j in range(TILE)]
        for u in range(t + 1, count):
            below = [along(strips[u], first + j) for j in range(TILE)]
            strips[u] = jnp.where(inside, 0.0, strips[u]) - combine(below, solved)
        if later:
            later.pop(0)()
    for call in later:
        call()
    return jnp.concatenate(done, axis=0)


def inverse_factor_kernel(gram_ref, inverse_ref, work_ref):
    count = gram_ref.shape[0] // LANES

    def at(i):
        return slice(LANES * i, LANES * (i + 1))

    square = (LANES, LANES)
    eye = lax.broadcasted_iota(jnp.int32, square, 0) == lax.broadcasted_iota(jnp.int32, square, 1)
    diagonal = [jnp.where(eye, gram_ref[at(i), at(i)], 0.0) for i in range(count)]
    by_lane = [lax.rsqrt(jnp.sum(d, axis=0, keepdims=True)) for d in diagonal]
    by_row = [lax.rsqrt(jnp.sum(d, axis=1, keepdims=True)) for d in diagonal]
    for i in range(count):
        for j in range(i, count):
            work_ref[at(i), at(j)] = gram_ref[at(i), at(j)] * by_row[i] * by_lane[j]
    inverse_ref[...] = jnp.zeros_like(inverse_ref)

    later = []
    for b in range(count):
        inverse = block_inverse(work_ref[at(b), at(b)], later)
        inverse_ref[at(b), at(b)] = inverse
        before = slice(0, LANES * b)
        factor = {}

        def finish(b=b, before=before, inverse=inverse):
            inverse_ref[at(b), before] = dot(inverse, work_ref[at(b), before], (1, 0))

        def strip(i, b=b, inverse=inverse, factor=factor):
            factor[i] = dot(inverse, work_ref[at(b), at(i)], (1, 0))

        def update(i, j, factor=factor):
            work_ref[at(i), at(j)] = work_ref[at(i), at(j)] - dot(factor[i], factor[j], (0, 0))

        def carry(i, b=b, inverse=inverse, factor=factor):
            work_ref[at(i), at(b)] = -dot(factor[i], inverse, (0, 0))

        def carry_before(i, b=b, before=before, factor=factor):
            work_ref[at(i), before] = work_ref[at(i), before] - dot(factor[i], inverse_ref[at(b), before], (0, 0))

        later = [finish] if b else []
        if b == count - 1:
            break
        strip(b + 1)
        update(b + 1, b + 1)
        later += [functools.partial(strip, i) for i in range(b + 2, count)]
        for i in range(b + 1, count):
            later += [functools.partial(update, i, j) for j in range(i, count) if (i, j) != (b + 1, b + 1)]
            later.append(functools.partial(carry, i))
            if b:
                later.append(functools.partial(carry_before, i))
    for call in later:
        call()
    for i in range(count):
        for j in range(i + 1):
            inverse_ref[at(i), at(j)] = inverse_ref[at(i), at(j)] * by_lane[j]


def inverse_factor(gram):
    return pl.pallas_call(
        inverse_factor_kernel,
        out_shape=jax.ShapeDtypeStruct(gram.shape, jnp.float32),
        in_specs=[pl.BlockSpec(memory_space=pltpu.VMEM)],
        out_specs=pl.BlockSpec(memory_space=pltpu.VMEM),
        scratch_shapes=[pltpu.VMEM(gram.shape, jnp.float32)],
        compiler_params=pltpu.CompilerParams(vmem_limit_bytes=16 * 1024 * 1024),
        cost_estimate=pl.CostEstimate(flops=1 << 30, bytes_accessed=1 << 26, transcendentals=0),
    )(gram)


def correct_kernel(left_ref, inverse_ref, right_ref, momentum_ref, gradient_ref, ortho_ref, next_ref):
    ortho = dot(inverse_ref[...], left_ref[...], (1, 0))
    ortho_ref[...] = ortho
    blend = momentum_ref[...] + gradient_ref[...].astype(jnp.float32)
    next_ref[...] = blend - 0.05 * dot(right_ref[...], ortho, (1, 0))


def correct(left, inverse, right, momentum, gradient):
    vmem = pl.BlockSpec(memory_space=pltpu.VMEM)
    return pl.pallas_call(
        correct_kernel,
        out_shape=(
            jax.ShapeDtypeStruct(left.shape, jnp.float32),
            jax.ShapeDtypeStruct(momentum.shape, jnp.float32),
        ),
        in_specs=[vmem] * 5,
        out_specs=(vmem, vmem),
        compiler_params=pltpu.CompilerParams(vmem_limit_bytes=24 * 1024 * 1024),
        cost_estimate=pl.CostEstimate(flops=1 << 33, bytes_accessed=1 << 23, transcendentals=0),
    )(left, inverse, right, momentum, gradient)


def sum_rows(block):
    share = lax.psum_scatter(block, "row", scatter_dimension=0, tiled=True)
    return lax.all_gather(share, "row", axis=0, tiled=True)


def shards(momentum, gradient, right_factor):
    rank = right_factor.shape[1]
    col = CHIPS + ("core",)
    blend = momentum + gradient.astype(jnp.float32)
    left = gather_columns(scatter(scatter(dot(right_factor, blend, (0, 1)), "core"), CHIPS))
    width = rank // lax.axis_size(col)
    position = lax.axis_index("core") * lax.axis_size(CHIPS) + lax.axis_index(CHIPS)
    mine = lax.dynamic_slice_in_dim(left, position * width, width, 0)
    piece = jnp.sum(spread(dot(mine, left, (1, 1))[None], "row"), axis=0)
    columns = blend.shape[1]
    spare = -columns % (TILE * lax.axis_size("row"))
    crossed = sum_rows(dot(jnp.pad(blend, ((0, 0), (0, spare))), left, (0, 1)))[:columns]
    inverse = inverse_factor(gather_columns(piece))
    right = dot(crossed, inverse, (1, 1))
    squares = jnp.sum(spread(jnp.sum(right * right, axis=0)[None], col), axis=0)
    total_cols = right.shape[0] * lax.axis_size(col)
    total_rows = blend.shape[0] * lax.axis_size("row")
    right_next = right * lax.rsqrt(squares / total_cols + 1e-06)
    ortho, momentum_next = correct(left, inverse, right, momentum.T, gradient.T)
    factor = jnp.sqrt(jnp.float32(total_rows) / rank)
    update = (factor * dot(right_next, ortho, (1, 0), HIGH)).astype(jnp.bfloat16)
    return (momentum_next.T, right_next, update.T)


def solution(mesh):
    rows = mesh.devices.shape[0]
    split = Mesh(mesh.devices.reshape(rows, 8, 4, 2), ("row", "y", "x", "core"))
    col = CHIPS + ("core",)
    return jax.shard_map(
        shards,
        mesh=split,
        in_specs=(P("row", col), P("row", col), P(col, None)),
        out_specs=(P("row", col), P(col, None), P("row", col)),
        check_vma=False,
    )
```

```python
import functools

import jax
import jax.numpy as jnp
from jax import lax
from jax.experimental import pallas as pl
from jax.experimental.pallas import tpu as pltpu
from jax.sharding import Mesh, PartitionSpec as P

HIGHEST = lax.Precision.HIGHEST
HIGH = lax.Precision.HIGH
CHIPS = ("y", "x")
TILE = 8
LANES = 128


def dot(a, b, dims, precision=HIGHEST):
    return lax.dot_general(
        a, b, ((dims[:1], dims[1:]), ((), ())), precision=precision, preferred_element_type=jnp.float32
    )


def exchange(blocks, axis):
    return lax.all_to_all(blocks, axis, 0, 0, tiled=True)


def spread(block, axis):
    copies = jnp.broadcast_to(block[None], (lax.axis_size(axis),) + block.shape)
    return exchange(copies, axis).reshape((-1,) + block.shape[1:])


def scatter(whole, axis):
    return jnp.sum(exchange(whole.reshape((lax.axis_size(axis), -1) + whole.shape[1:]), axis), axis=0)


def gather_columns(block):
    return spread(spread(block, CHIPS), "core")


def block_inverse(block, later):
    shape = (TILE, LANES)
    row = lax.broadcasted_iota(jnp.int32, shape, 0)
    lane = lax.broadcasted_iota(jnp.int32, shape, 1)
    at_row = [row == j for j in range(TILE)]

    def down(x, j):
        return jnp.broadcast_to(x[j : j + 1, :], shape)

    def along(x, k):
        return jnp.broadcast_to(x[:, k : k + 1], shape)

    def combine(columns, rows):
        terms = [c * r for c, r in zip(columns, rows)]
        while len(terms) > 1:
            terms = [terms[i] + terms[i + 1] for i in range(0, len(terms), 2)]
        return terms[0]

    later = list(later)
    count = LANES // TILE
    strips = [block[TILE * u : TILE * (u + 1), :] for u in range(count)]
    done = []
    for t in range(count):
        first = TILE * t
        inside = (lane >= first) & (lane < first + TILE)
        strip = strips[t]
        columns = [along(strip, first + j) for j in range(TILE)]
        rows = jnp.where(inside, jnp.where(lane - first == row, 1.0, 0.0), strip)
        rows = [down(rows, j) for j in range(TILE)]
        pivots = jnp.ones(shape, jnp.float32)
        lower = [jnp.where(at_row[m], 1.0, 0.0) for m in range(TILE)]
        for j in range(0, TILE, 2):
            k = j + 1
            upper_row = [down(columns[m], j) for m in range(TILE)]
            lower_row = [down(columns[m], k) for m in range(TILE)]
            a, b, d = upper_row[j], lower_row[j], lower_row[k]
            scale = 1.0 / (a * d - b * b)
            at_j = jnp.where(at_row[j], -1.0, jnp.where(at_row[k], 0.0, columns[j]))
            at_k = jnp.where(at_row[k], -1.0, jnp.where(at_row[j], 0.0, columns[k]))
            ratio_j = (at_j * d - at_k * b) * scale
            ratio_k = (at_k * a - at_j * b) * scale
            step = b / a
            pivots = jnp.where(at_row[j], a, jnp.where(at_row[k], d - b * step, pivots))
            for m in range(j):
                lower[m] = jnp.where(
                    at_row[j], upper_row[m], jnp.where(at_row[k], lower_row[m] - step * upper_row[m], lower[m])
                )
            lower[j] = jnp.where(at_row[k], -step, lower[j])
            pair = at_row[j] | at_row[k]
            columns = [
                -ratio_j
                if m == j
                else -ratio_k
                if m == k
                else (jnp.where(pair, 0.0, columns[m]) - ratio_j * upper_row[m]) - ratio_k * lower_row[m]
                for m in range(TILE)
            ]
        done.append(jnp.where(lane < first + TILE, combine(lower, rows) * lax.rsqrt(pivots), 0.0))
        solved = combine(columns, rows)
        solved = [down(solved, j) for j in range(TILE)]
        for u in range(t + 1, count):
            below = [along(strips[u], first + j) for j in range(TILE)]
            strips[u] = jnp.where(inside, 0.0, strips[u]) - combine(below, solved)
        if later:
            later.pop(0)()
    for call in later:
        call()
    return jnp.concatenate(done, axis=0)


def inverse_factor_kernel(gram_ref, inverse_ref, work_ref):
    count = gram_ref.shape[0] // LANES

    def at(i):
        return slice(LANES * i, LANES * (i + 1))

    def gram(i, j):
        row, slot = (i, j - i) if j - i < count - 1 else (count // 2, count - 2)
        return gram_ref[at(row), at(slot)]

    square = (LANES, LANES)
    eye = lax.broadcasted_iota(jnp.int32, square, 0) == lax.broadcasted_iota(jnp.int32, square, 1)
    diagonal = [jnp.where(eye, gram(i, i), 0.0) for i in range(count)]
    by_lane = [lax.rsqrt(jnp.sum(d, axis=0, keepdims=True)) for d in diagonal]
    by_row = [lax.rsqrt(jnp.sum(d, axis=1, keepdims=True)) for d in diagonal]
    for i in range(count):
        for j in range(i, count):
            work_ref[at(i), at(j)] = gram(i, j) * by_row[i] * by_lane[j]
    inverse_ref[...] = jnp.zeros_like(inverse_ref)

    later = []
    for b in range(count):
        inverse = block_inverse(work_ref[at(b), at(b)], later)
        inverse_ref[at(b), at(b)] = inverse
        before = slice(0, LANES * b)
        factor = {}

        def finish(b=b, before=before, inverse=inverse):
            inverse_ref[at(b), before] = dot(inverse, work_ref[at(b), before], (1, 0))

        def strip(i, b=b, inverse=inverse, factor=factor):
            factor[i] = dot(inverse, work_ref[at(b), at(i)], (1, 0))

        def update(i, j, factor=factor):
            work_ref[at(i), at(j)] = work_ref[at(i), at(j)] - dot(factor[i], factor[j], (0, 0))

        def carry(i, b=b, inverse=inverse, factor=factor):
            work_ref[at(i), at(b)] = -dot(factor[i], inverse, (0, 0))

        def carry_before(i, b=b, before=before, factor=factor):
            work_ref[at(i), before] = work_ref[at(i), before] - dot(factor[i], inverse_ref[at(b), before], (0, 0))

        later = [finish] if b else []
        if b == count - 1:
            break
        strip(b + 1)
        update(b + 1, b + 1)
        later += [functools.partial(strip, i) for i in range(b + 2, count)]
        for i in range(b + 1, count):
            later += [functools.partial(update, i, j) for j in range(i, count) if (i, j) != (b + 1, b + 1)]
            later.append(functools.partial(carry, i))
            if b:
                later.append(functools.partial(carry_before, i))
    for call in later:
        call()
    for i in range(count):
        for j in range(i + 1):
            inverse_ref[at(i), at(j)] = inverse_ref[at(i), at(j)] * by_lane[j]


def inverse_factor(packed):
    square = (packed.shape[0], packed.shape[0])
    return pl.pallas_call(
        inverse_factor_kernel,
        out_shape=jax.ShapeDtypeStruct(square, jnp.float32),
        in_specs=[pl.BlockSpec(memory_space=pltpu.VMEM)],
        out_specs=pl.BlockSpec(memory_space=pltpu.VMEM),
        scratch_shapes=[pltpu.VMEM(square, jnp.float32)],
        compiler_params=pltpu.CompilerParams(vmem_limit_bytes=16 * 1024 * 1024),
        cost_estimate=pl.CostEstimate(flops=1 << 30, bytes_accessed=1 << 26, transcendentals=0),
    )(packed)


def pack_strip(left, position):
    count = left.shape[0] // LANES
    strips = LANES // TILE
    level = position // strips
    other = position - strips * (count // 2)
    mine = lax.dynamic_slice_in_dim(left, position * TILE, TILE, 0)
    borrowed = lax.dynamic_slice_in_dim(left, jnp.maximum(other, 0) * TILE, TILE, 0)
    product = dot(jnp.concatenate([mine, borrowed], axis=0), left, (1, 1))
    blocks = [product[:TILE, LANES * j : LANES * (j + 1)] for j in range(count)]
    slots = []
    for slot in range(count - 1):
        choice = blocks[count - 1]
        for i in range(count - 1 - slot):
            choice = jnp.where(level == i, blocks[i + slot], choice)
        slots.append(choice)
    slots[-1] = jnp.where(level == count // 2, product[TILE:, LANES * (count - 1) :], slots[-1])
    return jnp.concatenate(slots, axis=1)


def correct_kernel(left_ref, inverse_ref, right_ref, momentum_ref, gradient_ref, ortho_ref, next_ref):
    ortho = dot(inverse_ref[...], left_ref[...], (1, 0))
    ortho_ref[...] = ortho
    blend = momentum_ref[...] + gradient_ref[...].astype(jnp.float32)
    next_ref[...] = blend - 0.05 * dot(right_ref[...], ortho, (1, 0))


def correct(left, inverse, right, momentum, gradient):
    vmem = pl.BlockSpec(memory_space=pltpu.VMEM)
    return pl.pallas_call(
        correct_kernel,
        out_shape=(
            jax.ShapeDtypeStruct(left.shape, jnp.float32),
            jax.ShapeDtypeStruct(momentum.shape, jnp.float32),
        ),
        in_specs=[vmem] * 5,
        out_specs=(vmem, vmem),
        compiler_params=pltpu.CompilerParams(vmem_limit_bytes=24 * 1024 * 1024),
        cost_estimate=pl.CostEstimate(flops=1 << 33, bytes_accessed=1 << 23, transcendentals=0),
    )(left, inverse, right, momentum, gradient)


def sum_rows(block):
    share = lax.psum_scatter(block, "row", scatter_dimension=0, tiled=True)
    return lax.all_gather(share, "row", axis=0, tiled=True)


def shards(momentum, gradient, right_factor):
    rank = right_factor.shape[1]
    col = CHIPS + ("core",)
    blend = momentum + gradient.astype(jnp.float32)
    left = gather_columns(scatter(scatter(dot(right_factor, blend, (0, 1)), "core"), CHIPS))
    position = lax.axis_index("core") * lax.axis_size(CHIPS) + lax.axis_index(CHIPS)
    piece = jnp.sum(spread(pack_strip(left, position)[None], "row"), axis=0)
    columns = blend.shape[1]
    spare = -columns % (TILE * lax.axis_size("row"))
    crossed = sum_rows(dot(jnp.pad(blend, ((0, 0), (0, spare))), left, (0, 1)))[:columns]
    inverse = inverse_factor(gather_columns(piece))
    right = dot(crossed, inverse, (1, 1))
    squares = jnp.sum(spread(jnp.sum(right * right, axis=0)[None], col), axis=0)
    total_cols = right.shape[0] * lax.axis_size(col)
    total_rows = blend.shape[0] * lax.axis_size("row")
    right_next = right * lax.rsqrt(squares / total_cols + 1e-06)
    ortho, momentum_next = correct(left, inverse, right, momentum.T, gradient.T)
    factor = jnp.sqrt(jnp.float32(total_rows) / rank)
    update = (factor * dot(right_next, ortho, (1, 0), HIGH)).astype(jnp.bfloat16)
    return (momentum_next.T, right_next, update.T)


def solution(mesh):
    rows = mesh.devices.shape[0]
    split = Mesh(mesh.devices.reshape(rows, 8, 4, 2), ("row", "y", "x", "core"))
    col = CHIPS + ("core",)
    return jax.shard_map(
        shards,
        mesh=split,
        in_specs=(P("row", col), P("row", col), P(col, None)),
        out_specs=(P("row", col), P(col, None), P("row", col)),
        check_vma=False,
    )
```

```python
import functools

import jax
import jax.numpy as jnp
from jax import lax
from jax.experimental import pallas as pl
from jax.experimental.pallas import tpu as pltpu
from jax.sharding import Mesh, PartitionSpec as P

HIGHEST = lax.Precision.HIGHEST
HIGH = lax.Precision.HIGH
CHIPS = ("y", "x")
TILE = 8
LANES = 128


def dot(a, b, dims, precision=HIGHEST):
    return lax.dot_general(
        a, b, ((dims[:1], dims[1:]), ((), ())), precision=precision, preferred_element_type=jnp.float32
    )


def exchange(blocks, axis):
    return lax.all_to_all(blocks, axis, 0, 0, tiled=True)


def spread(block, axis):
    copies = jnp.broadcast_to(block[None], (lax.axis_size(axis),) + block.shape)
    return exchange(copies, axis).reshape((-1,) + block.shape[1:])


def scatter(whole, axis):
    return jnp.sum(exchange(whole.reshape((lax.axis_size(axis), -1) + whole.shape[1:]), axis), axis=0)


def gather_columns(block):
    return spread(spread(block, CHIPS), "core")


def block_inverse(block, later):
    shape = (TILE, LANES)
    row = lax.broadcasted_iota(jnp.int32, shape, 0)
    lane = lax.broadcasted_iota(jnp.int32, shape, 1)
    at_row = [row == j for j in range(TILE)]

    def down(x, j):
        return jnp.broadcast_to(x[j : j + 1, :], shape)

    def along(x, k):
        return jnp.broadcast_to(x[:, k : k + 1], shape)

    def combine(columns, rows):
        terms = [c * r for c, r in zip(columns, rows)]
        while len(terms) > 1:
            terms = [terms[i] + terms[i + 1] for i in range(0, len(terms), 2)]
        return terms[0]

    later = list(later)
    count = LANES // TILE
    strips = [block[TILE * u : TILE * (u + 1), :] for u in range(count)]
    done = []
    for t in range(count):
        first = TILE * t
        inside = (lane >= first) & (lane < first + TILE)
        strip = strips[t]
        columns = [along(strip, first + j) for j in range(TILE)]
        rows = jnp.where(inside, jnp.where(lane - first == row, 1.0, 0.0), strip)
        rows = [down(rows, j) for j in range(TILE)]
        pivots = jnp.ones(shape, jnp.float32)
        lower = [jnp.where(at_row[m], 1.0, 0.0) for m in range(TILE)]
        for j in range(0, TILE, 2):
            k = j + 1
            upper_row = [down(columns[m], j) for m in range(TILE)]
            lower_row = [down(columns[m], k) for m in range(TILE)]
            a, b, d = upper_row[j], lower_row[j], lower_row[k]
            scale = 1.0 / (a * d - b * b)
            at_j = jnp.where(at_row[j], -1.0, jnp.where(at_row[k], 0.0, columns[j]))
            at_k = jnp.where(at_row[k], -1.0, jnp.where(at_row[j], 0.0, columns[k]))
            ratio_j = (at_j * d - at_k * b) * scale
            ratio_k = (at_k * a - at_j * b) * scale
            step = b / a
            pivots = jnp.where(at_row[j], a, jnp.where(at_row[k], d - b * step, pivots))
            for m in range(j):
                lower[m] = jnp.where(
                    at_row[j], upper_row[m], jnp.where(at_row[k], lower_row[m] - step * upper_row[m], lower[m])
                )
            lower[j] = jnp.where(at_row[k], -step, lower[j])
            pair = at_row[j] | at_row[k]
            columns = [
                -ratio_j
                if m == j
                else -ratio_k
                if m == k
                else (jnp.where(pair, 0.0, columns[m]) - ratio_j * upper_row[m]) - ratio_k * lower_row[m]
                for m in range(TILE)
            ]
        done.append(jnp.where(lane < first + TILE, combine(lower, rows) * lax.rsqrt(pivots), 0.0))
        solved = combine(columns, rows)
        solved = [down(solved, j) for j in range(TILE)]
        for u in range(t + 1, count):
            below = [along(strips[u], first + j) for j in range(TILE)]
            strips[u] = jnp.where(inside, 0.0, strips[u]) - combine(below, solved)
        if later:
            later.pop(0)()
    for call in later:
        call()
    return jnp.concatenate(done, axis=0)


def inverse_factor_kernel(gram_ref, inverse_ref, work_ref):
    count = gram_ref.shape[0] // LANES

    def at(i):
        return slice(LANES * i, LANES * (i + 1))

    def gram(i, j):
        row, slot = (i, j - i) if j - i < count - 1 else (count // 2, count - 2)
        return gram_ref[at(row), at(slot)]

    square = (LANES, LANES)
    eye = lax.broadcasted_iota(jnp.int32, square, 0) == lax.broadcasted_iota(jnp.int32, square, 1)
    diagonal = [jnp.where(eye, gram(i, i), 0.0) for i in range(count)]
    by_lane = [lax.rsqrt(jnp.sum(d, axis=0, keepdims=True)) for d in diagonal]
    by_row = [lax.rsqrt(jnp.sum(d, axis=1, keepdims=True)) for d in diagonal]
    for i in range(count):
        for j in range(i, count):
            work_ref[at(i), at(j)] = gram(i, j) * by_row[i] * by_lane[j]
    inverse_ref[...] = jnp.zeros_like(inverse_ref)

    later = []
    for b in range(count):
        inverse = block_inverse(work_ref[at(b), at(b)], later)
        inverse_ref[at(b), at(b)] = inverse
        before = slice(0, LANES * b)
        factor = {}

        def finish(b=b, before=before, inverse=inverse):
            inverse_ref[at(b), before] = dot(inverse, work_ref[at(b), before], (1, 0))

        def strip(i, b=b, inverse=inverse, factor=factor):
            factor[i] = dot(inverse, work_ref[at(b), at(i)], (1, 0))

        def update(i, j, factor=factor):
            work_ref[at(i), at(j)] = work_ref[at(i), at(j)] - dot(factor[i], factor[j], (0, 0))

        def carry(i, b=b, inverse=inverse, factor=factor):
            work_ref[at(i), at(b)] = -dot(factor[i], inverse, (0, 0))

        def carry_before(i, b=b, before=before, factor=factor):
            work_ref[at(i), before] = work_ref[at(i), before] - dot(factor[i], inverse_ref[at(b), before], (0, 0))

        later = [finish] if b else []
        if b == count - 1:
            break
        strip(b + 1)
        update(b + 1, b + 1)
        later += [functools.partial(strip, i) for i in range(b + 2, count)]
        for i in range(b + 1, count):
            later += [functools.partial(update, i, j) for j in range(i, count) if (i, j) != (b + 1, b + 1)]
            later.append(functools.partial(carry, i))
            if b:
                later.append(functools.partial(carry_before, i))
    for call in later:
        call()
    for i in range(count):
        for j in range(i + 1):
            inverse_ref[at(i), at(j)] = inverse_ref[at(i), at(j)] * by_lane[j]


def inverse_factor(packed):
    square = (packed.shape[0], packed.shape[0])
    return pl.pallas_call(
        inverse_factor_kernel,
        out_shape=jax.ShapeDtypeStruct(square, jnp.float32),
        in_specs=[pl.BlockSpec(memory_space=pltpu.VMEM)],
        out_specs=pl.BlockSpec(memory_space=pltpu.VMEM),
        scratch_shapes=[pltpu.VMEM(square, jnp.float32)],
        compiler_params=pltpu.CompilerParams(vmem_limit_bytes=16 * 1024 * 1024),
        cost_estimate=pl.CostEstimate(flops=1 << 30, bytes_accessed=1 << 26, transcendentals=0),
    )(packed)


def pack_strip(left, position):
    count = left.shape[0] // LANES
    strips = LANES // TILE
    level = position // strips
    other = position - strips * (count // 2)
    mine = lax.dynamic_slice_in_dim(left, position * TILE, TILE, 0)
    borrowed = lax.dynamic_slice_in_dim(left, jnp.maximum(other, 0) * TILE, TILE, 0)
    product = dot(jnp.concatenate([mine, borrowed], axis=0), left, (1, 1))
    blocks = [product[:TILE, LANES * j : LANES * (j + 1)] for j in range(count)]
    slots = []
    for slot in range(count - 1):
        choice = blocks[count - 1]
        for i in range(count - 1 - slot):
            choice = jnp.where(level == i, blocks[i + slot], choice)
        slots.append(choice)
    slots[-1] = jnp.where(level == count // 2, product[TILE:, LANES * (count - 1) :], slots[-1])
    return jnp.concatenate(slots, axis=1)


def correct_kernel(left_ref, inverse_ref, right_ref, momentum_ref, gradient_ref, ortho_ref, next_ref):
    ortho = dot(inverse_ref[...], left_ref[...], (1, 0))
    ortho_ref[...] = ortho
    blend = momentum_ref[...] + gradient_ref[...].astype(jnp.float32)
    next_ref[...] = blend - 0.05 * dot(right_ref[: next_ref.shape[0], :], ortho, (1, 0))


def correct(left, inverse, right, momentum, gradient):
    vmem = pl.BlockSpec(memory_space=pltpu.VMEM)
    return pl.pallas_call(
        correct_kernel,
        out_shape=(
            jax.ShapeDtypeStruct(left.shape, jnp.float32),
            jax.ShapeDtypeStruct(momentum.shape, jnp.float32),
        ),
        in_specs=[vmem] * 5,
        out_specs=(vmem, vmem),
        compiler_params=pltpu.CompilerParams(vmem_limit_bytes=24 * 1024 * 1024),
        cost_estimate=pl.CostEstimate(flops=1 << 33, bytes_accessed=1 << 23, transcendentals=0),
    )(left, inverse, right, momentum, gradient)


def shards(momentum, gradient, right_factor):
    rank = right_factor.shape[1]
    col = CHIPS + ("core",)
    blend = momentum + gradient.astype(jnp.float32)
    left = gather_columns(scatter(scatter(dot(right_factor, blend, (0, 1)), "core"), CHIPS))
    position = lax.axis_index("core") * lax.axis_size(CHIPS) + lax.axis_index(CHIPS)
    piece = jnp.sum(spread(pack_strip(left, position)[None], "row"), axis=0)
    columns = blend.shape[1]
    spare = -columns % (TILE * lax.axis_size("row"))
    crossed = dot(jnp.pad(blend, ((0, 0), (0, spare))), left, (0, 1))
    share = lax.psum_scatter(crossed, "row", scatter_dimension=0, tiled=True)
    inverse = inverse_factor(gather_columns(piece))
    right = lax.all_gather(dot(share, inverse, (1, 1)), "row", axis=0, tiled=True)
    squares = jnp.sum(right * right, axis=0).reshape(1, -1, LANES)
    squares = jnp.sum(spread(squares, col), axis=0).reshape(rank)
    total_cols = columns * lax.axis_size(col)
    total_rows = blend.shape[0] * lax.axis_size("row")
    right_next = right[:columns] * lax.rsqrt(squares / total_cols + 1e-06)
    ortho, momentum_next = correct(left, inverse, right, momentum.T, gradient.T)
    factor = jnp.sqrt(jnp.float32(total_rows) / rank)
    update = (factor * dot(right_next, ortho, (1, 0), HIGH)).astype(jnp.bfloat16)
    return (momentum_next.T, right_next, update.T)


def solution(mesh):
    rows = mesh.devices.shape[0]
    split = Mesh(mesh.devices.reshape(rows, 8, 4, 2), ("row", "y", "x", "core"))
    col = CHIPS + ("core",)
    return jax.shard_map(
        shards,
        mesh=split,
        in_specs=(P("row", col), P("row", col), P(col, None)),
        out_specs=(P("row", col), P(col, None), P("row", col)),
        check_vma=False,
    )
```
